256 devices in a mesh: rep: 8 (over x, core), tensor: 32 (over z, y).
Axes of the slice: x: 4, y: 4, z: 8, core: 2. Of those that a mesh axis runs over, the one named last changes fastest.
Arguments:
- amplitudes: bfloat16 [2048, 8, 8192], P('tensor', None, 'rep'), may hold values from -6 to 6
- integrals: bfloat16 [32, 2048, 8192], P('tensor', None, 'rep'), as said below
- rest: bfloat16 [2048, 8, 8192], P('tensor', None, 'rep'), may hold values from -6 to 6
- occ_energy: float32 [2048], P('tensor'), may hold values from -2 to -0.4
- virt_energy: float32 [8, 8192], P(None, 'rep'), may hold values from 0.4 to 2
- sizes: int32 [8], replicated, may hold values from 4096 to 8192, as said below
- order: int32 [8], replicated, may hold values from 0 to 7, each once
Outputs:
- new_amplitudes: bfloat16 [2048, 8, 8192], P('tensor', None, 'rep')
The draws below stay inside these ranges and needn't reach their ends.
Inputs may be any that keep to these rules, and one draw needn't show every extreme that they name: `sizes`: each is a multiple of 128, and one sector holds exactly 8192. `order`: each sector once. `integrals`: each slot's block V_k is symmetric, V_k[x, y] = V_k[y, x].
All inputs are finite; a program needn't handle non-finite values.
Results may differ from the reference program's by a relative error of at most 0.001.
Values may be sent and summed in bfloat16 or wider, within the bound.
A program may use at most 128 MiB of HBM per device.

```python
import jax
import jax.numpy as jnp
from jax import lax

CAP = 8192
G = 8
Q = 4
PIECE = 256
IJ = 2048
N_REP = 8


def draw_integrals(key, part):
    key = jax.random.fold_in(key, 11)
    base = jax.random.normal(key, (G, CAP, CAP), jnp.float32)
    both = (base + jnp.swapaxes(base, 1, 2)) * 0.5 ** 0.5 / CAP ** 0.5
    arranged = jnp.transpose(both.reshape(G, N_REP, Q, PIECE, CAP), (0, 2, 1, 3, 4)).reshape(G * Q, CAP // Q, CAP)
    return arranged.astype(jnp.bfloat16)


def draw_sizes(key, part):
    key = jax.random.fold_in(key, 23)
    first, second = jax.random.split(key)
    granule = CAP // 64
    counts = jax.random.randint(first, (G,), 32, 65, dtype=jnp.int32) * granule
    place = jax.random.randint(second, (), 0, G, dtype=jnp.int32)
    return counts.at[place].set(CAP)


def levels(rng, shape, shards, low, top_value):
    def one(dim, blocks):
        steps = jax.random.uniform(jax.random.fold_in(jax.random.fold_in(rng, 6), dim), (blocks,), jnp.float32, low / len(shards), top_value / len(shards))
        return jnp.repeat(jnp.exp(steps), shape[dim] // blocks).reshape((-1,) + (1,) * (len(shape) - dim - 1))

    loudness = one(*shards[0])
    for cut in shards[1:]:
        loudness = loudness * one(*cut)
    return loudness


def noise(own_key, extent, spread, reach, cuts=(), kind=jnp.bfloat16):
    drawn = jax.random.normal(own_key, extent, jnp.float32) * spread
    if len(cuts) > 0:
        drawn = levels(own_key, extent, cuts, -0.22, 0.18) * drawn
    return jnp.clip(drawn, min=-reach, max=reach).astype(kind)


def setup_inputs(seed: int = 0) -> dict:
    arg_keys = jax.random.split(jax.random.key(seed), 8)
    return {
        "amplitudes": noise(arg_keys[0], (IJ, G, CAP), 1.0, 6.0, ((0, 32), (2, 8))),
        "integrals": draw_integrals(jax.random.fold_in(arg_keys[7], 71), 0),
        "rest": noise(arg_keys[2], (IJ, G, CAP), 1.0, 6.0, ((0, 32), (2, 8))),
        "occ_energy": jnp.clip(-2.0 + 1.6 * jax.random.uniform(arg_keys[3], (IJ,), jnp.float32) ** levels(arg_keys[3], (IJ,), ((0, 32),), -0.2, 0.2), -2.0, -0.4),
        "virt_energy": jnp.clip(0.4 + 1.6 * jax.random.uniform(arg_keys[4], (G, CAP), jnp.float32) ** levels(arg_keys[4], (G, CAP), ((1, 8),), -0.2, 0.2), 0.4, 2.0),
        "sizes": draw_sizes(jax.random.fold_in(arg_keys[7], 71), 0),
        "order": jax.random.permutation(arg_keys[6], G).astype(jnp.int32),
    }


def reference(amplitudes, integrals, rest, occ_energy, virt_energy, sizes, order):
    groups = amplitudes.shape[1]
    cap = amplitudes.shape[2]
    column = jnp.arange(cap, dtype=jnp.int32)
    keep = column[None, :] < sizes[:, None]
    masked = jnp.where(keep[None], amplitudes, jnp.zeros((), amplitudes.dtype))

    def one_slot(slot):
        sector = order[slot]
        block = lax.dynamic_index_in_dim(masked, sector, 1, keepdims=False)
        banded = lax.dynamic_slice_in_dim(integrals, (slot * Q).astype(jnp.int32), Q, 0)
        coupling = jnp.transpose(banded.reshape(Q, N_REP, PIECE, cap), (1, 0, 2, 3)).reshape(cap, cap)
        return jnp.dot(block, coupling.T, preferred_element_type=jnp.float32)

    stacked = lax.map(one_slot, jnp.arange(groups, dtype=jnp.int32))
    positions = jnp.arange(groups, dtype=jnp.int32)
    inverse = jnp.sum(jnp.where(order[None, :] == positions[:, None], positions[None, :], 0), axis=1).astype(jnp.int32)
    ladder = jnp.transpose(jnp.take(stacked, inverse, axis=0), (1, 0, 2))
    denom = occ_energy[:, None, None] - virt_energy[None]
    update = (ladder + rest.astype(jnp.float32)) / denom
    return jnp.where(keep[None], update, jnp.zeros((), jnp.float32)).astype(jnp.bfloat16)
```

```python
import jax
import jax.numpy as jnp
from jax import lax
from jax.experimental import pallas as pl
from jax.experimental.pallas import tpu as pltpu
from jax.sharding import PartitionSpec as P

MESH = pl.DeviceIdType.MESH
NX, NY, NZ = 4, 4, 8
F32, BF16 = jnp.float32, jnp.bfloat16


def dot_t(a, b):
    return lax.dot_general(a, b, (((1,), (1,)), ((), ())), preferred_element_type=F32)


def kernel(
    amp_ref, int_ref, rest_ref, occ_ref, virt_ref, sizes_ref, order_ref, out_ref,
    slots, rest_slots, a_own, a_oth, v_own, v_oth, part, relay_l, relay_r, from_l, from_r, lad, upd,
    zs, zr, ys, yr, cs, cr, vs, vr, vl, xs, xr, rs, rr,
):
    rep, tensor = lax.axis_index("rep"), lax.axis_index("tensor")
    x, core = rep // 2, rep % 2
    z, y = tensor // NY, tensor % NY
    rows, width = amp_ref.shape[0] // NZ, amp_ref.shape[1]
    block = rows * NZ
    half = block // 2
    piece = width // NY

    def at_x(step):
        return lax.rem(x + step + NX, NX) * 2 + core

    def at_y(step):
        return z * NY + lax.rem(y + step + NY, NY)

    other = x * 2 + 1 - core

    def copy(src, dst, send, recv, to_rep, to_tensor):
        return pltpu.make_async_remote_copy(
            src_ref=src, dst_ref=dst, send_sem=send, recv_sem=recv,
            device_id=(to_rep, to_tensor), device_id_type=MESH,
        )

    barrier = pltpu.get_barrier_semaphore()

    def peer(dz, dy):
        return lax.rem(z + dz, NZ) * NY + lax.rem(y + dy, NY)

    for dz in range(NZ):
        for dy in range(NY):
            if dz or dy:
                pl.semaphore_signal(barrier, inc=1, device_id=(rep, peer(dz, dy)), device_id_type=MESH)
    for to in (at_x(1), at_x(-1), other):
        pl.semaphore_signal(barrier, inc=1, device_id=(to, tensor), device_id_type=MESH)

    v_local = pltpu.make_async_copy(int_ref.at[:, core], v_own, vl)
    v_local.start()

    line = lax.broadcasted_iota(jnp.int32, (rows, block), 1)
    which = lax.broadcasted_iota(jnp.int32, (rows, block), 0)
    column = rep * width + lax.broadcasted_iota(jnp.int32, (rows, width), 1)
    amp, rest = amp_ref[...], rest_ref[...]
    for k in range(NZ):
        sector = order_ref[k]
        pick = jnp.where(line == which * NZ + sector, 1.0, 0.0).astype(BF16)
        moved = jnp.dot(pick, amp, preferred_element_type=F32)
        slots[k] = jnp.where(column < sizes_ref[sector], moved, 0.0).astype(BF16)

    pl.semaphore_wait(barrier, NZ * NY - 1 + 3)

    z_copies = []
    for dz in (4, 3, 5, 2, 6, 1, 7):
        to = lax.rem(z + dz, NZ)
        c = copy(
            slots.at[to], a_own.at[0, pl.ds(pl.multiple_of(z * rows, rows), rows)],
            zs.at[dz], zr.at[dz], rep, to * NY + y,
        )
        c.start()
        z_copies.append(c)
    v_copy = copy(int_ref.at[:, 1 - core], v_oth, vs, vr, other, tensor)
    v_copy.start()
    a_own[0, pl.ds(pl.multiple_of(z * rows, rows), rows), :] = slots[z]

    for k in range(NZ):
        pick = jnp.where(line == which * NZ + order_ref[k], 1.0, 0.0).astype(BF16)
        moved = jnp.dot(pick, rest, preferred_element_type=F32)
        rest_slots[k] = moved.astype(BF16)

    upper, lower = pl.ds(0, half), pl.ds(half, half)
    y_copies = [
        copy(a_own.at[0], a_own.at[3], ys.at[0], yr.at[0], rep, at_y(1)),
        copy(a_own.at[0], a_own.at[1], ys.at[1], yr.at[1], rep, at_y(-1)),
        copy(a_own.at[3, upper], a_own.at[2, upper], ys.at[2], yr.at[2], rep, at_y(1)),
        copy(a_own.at[1, lower], a_own.at[2, lower], ys.at[3], yr.at[3], rep, at_y(-1)),
    ]
    c_copies = [copy(a_own.at[d], a_oth.at[d], cs.at[d], cr.at[d], other, tensor) for d in range(NY)]
    x_copies = [
        [
            copy(part.at[d, 2, upper], relay_l.at[d], xs.at[d, 0], xr.at[d, 0], at_x(1), tensor),
            copy(part.at[d, 2, lower], relay_r.at[d], xs.at[d, 1], xr.at[d, 1], at_x(-1), tensor),
            copy(part.at[d, 1], from_l.at[d], xs.at[d, 2], xr.at[d, 2], at_x(1), tensor),
            copy(part.at[d, 3], from_r.at[d], xs.at[d, 3], xr.at[d, 3], at_x(-1), tensor),
        ]
        for d in range(NY)
    ]
    r_copies = {}

    def compute(d, s):
        t = lax.rem(x + s, NX)

        @pl.loop(0, 2)
        def _(m):
            here = pl.ds(pl.multiple_of(m * half, half), half)
            part[d, s, here, :] = dot_t(a_own[d, here, :], v_own[t]) + dot_t(a_oth[d, here, :], v_oth[t])

    def chunk(d):
        c_copies[d].wait_recv()
        compute(d, 2)
        x_copies[d][0].start()
        x_copies[d][1].start()
        compute(d, 1)
        compute(d, 3)
        x_copies[d][0].wait_recv()
        part[d, 1, upper, :] += relay_l[d]
        x_copies[d][2].start()
        x_copies[d][1].wait_recv()
        part[d, 3, lower, :] += relay_r[d]
        x_copies[d][3].start()
        compute(d, 0)

    def finish(d):
        x_copies[d][2].wait_recv()
        x_copies[d][3].wait_recv()
        part[d, 0] += from_l[d] + from_r[d]
        for dz in range(NZ):
            to = lax.rem(z + dz, NZ)
            src = part.at[d, 0, pl.ds(pl.multiple_of(to * rows, rows), rows)]
            if dz or d:
                i = dz * NY + d
                c = copy(src, lad.at[z, y], rs.at[i], rr.at[i], rep, peer(dz, d))
                c.start()
                r_copies[i] = c
            else:
                lad[z, y] = part[d, 0, pl.ds(pl.multiple_of(z * rows, rows), rows), :]

    for c in z_copies:
        c.wait_recv()
    y_copies[0].start()
    y_copies[1].start()
    c_copies[0].start()
    v_local.wait()
    v_copy.wait_recv()
    chunk(0)
    y_copies[0].wait_recv()
    y_copies[2].start()
    c_copies[3].start()
    y_copies[1].wait_recv()
    y_copies[3].start()
    c_copies[1].start()
    chunk(3)
    finish(0)
    chunk(1)
    y_copies[2].wait_recv()
    y_copies[3].wait_recv()
    c_copies[2].start()
    finish(3)
    chunk(2)
    finish(1)
    finish(2)

    for c in r_copies.values():
        c.wait_recv()
    eye = lax.broadcasted_iota(jnp.int32, (rows, rows), 0) == lax.broadcasted_iota(jnp.int32, (rows, rows), 1)
    occ = jnp.sum(jnp.where(eye, occ_ref[...], 0.0), axis=1, keepdims=True)
    for k in range(NZ):
        sector = order_ref[k]
        virt = virt_ref[pl.ds(sector, 1), :]
        for c in range(NY):
            cols = slice(c * piece, (c + 1) * piece)
            new = (lad[k, c] + rest_slots[k, :, cols].astype(F32)) / (occ - virt[:, cols])
            new = jnp.where(column[:, cols] < sizes_ref[sector], new, 0.0)
            upd[k * rows : (k + 1) * rows, cols] = new.astype(BF16)

    wide = lax.broadcasted_iota(jnp.int32, (1, block), 1)
    lane = jnp.zeros((1, block), jnp.int32)
    for k in range(NZ):
        lane = jnp.where(wide // rows == k, (wide - k * rows) * NZ + order_ref[k], lane)
    back = jnp.where(lax.broadcasted_iota(jnp.int32, (block, block), 0) == lane, 1.0, 0.0).astype(BF16)
    out_ref[...] = jnp.dot(back, upd[...], preferred_element_type=F32).astype(BF16)

    v_copy.wait_send()
    for c in z_copies + y_copies + c_copies + sum(x_copies, []) + list(r_copies.values()):
        c.wait_send()


def on_device(amplitudes, integrals, rest, occ_energy, virt_energy, sizes, order):
    rows, groups, width = amplitudes.shape
    piece = width // NY
    block = rows * groups
    vmem, smem = pl.BlockSpec(memory_space=pltpu.VMEM), pl.BlockSpec(memory_space=pltpu.SMEM)
    dma = pltpu.SemaphoreType.DMA
    out = pl.pallas_call(
        kernel,
        out_shape=jax.ShapeDtypeStruct((block, width), BF16),
        in_specs=[vmem, pl.BlockSpec(memory_space=pl.ANY), vmem, vmem, vmem, smem, smem],
        out_specs=vmem,
        scratch_shapes=[
            pltpu.VMEM((NZ, rows, width), BF16),
            pltpu.VMEM((NZ, rows, width), BF16),
            pltpu.VMEM((NY, block, width), BF16),
            pltpu.VMEM((NY, block, width), BF16),
            pltpu.VMEM((NX, piece, width), BF16),
            pltpu.VMEM((NX, piece, width), BF16),
            pltpu.VMEM((NY, NX, block, piece), F32),
            pltpu.VMEM((NY, block // 2, piece), F32),
            pltpu.VMEM((NY, block // 2, piece), F32),
            pltpu.VMEM((NY, block, piece), F32),
            pltpu.VMEM((NY, block, piece), F32),
            pltpu.VMEM((NZ, NY, rows, piece), F32),
            pltpu.VMEM((block, width), BF16),
            dma((NZ,)), dma((NZ,)), dma((4,)), dma((4,)), dma((NY,)), dma((NY,)),
            dma(()), dma(()), dma(()),
            dma((NY, 4)), dma((NY, 4)), dma((NZ * NY,)), dma((NZ * NY,)),
        ],
        compiler_params=pltpu.CompilerParams(
            collective_id=0, has_side_effects=True, vmem_limit_bytes=56 * 2**20
        ),
        cost_estimate=pl.CostEstimate(flops=2 * 2048 * 2048 * 1024, bytes_accessed=8 << 20, transcendentals=0),
    )(
        amplitudes.reshape(block, width),
        integrals.reshape(NX, 2, piece, width),
        rest.reshape(block, width),
        occ_energy.reshape(1, rows),
        virt_energy,
        sizes,
        order,
    )
    return out.reshape(rows, groups, width)


def solution(mesh):
    placed = (
        P("tensor", None, "rep"),
        P("tensor", None, "rep"),
        P("tensor", None, "rep"),
        P("tensor"),
        P(None, "rep"),
        P(),
        P(),
    )
    return jax.shard_map(
        on_device, mesh=mesh, in_specs=placed, out_specs=P("tensor", None, "rep"), check_vma=False
    )
```

```python
import jax
import jax.numpy as jnp
from jax import lax
from jax.experimental import pallas as pl
from jax.experimental.pallas import tpu as pltpu
from jax.sharding import PartitionSpec as P

MESH = pl.DeviceIdType.MESH
NX, NY, NZ = 4, 4, 8
F32, BF16, I16, I32 = jnp.float32, jnp.bfloat16, jnp.int16, jnp.int32
PARTS = 2
LANES = 128
PER = 16
LN = 0.6931471805599453 / PER


def dot_t(a, b):
    return lax.dot_general(a, b, (((1,), (1,)), ((), ())), preferred_element_type=F32)


def scale_of(grouped):
    most = jnp.maximum(jnp.max(jnp.abs(grouped), axis=0), 1e-30)
    return (jnp.log(most) * (1 / LN) + (128 * PER + 1.02)).astype(I32) - 128 * PER


def fixed(grouped, code):
    return (grouped * jnp.exp((15 * PER - code).astype(F32) * LN)[None] + 32768.5).astype(I32) - 32768


def encode(ref, values):
    grouped = [v.reshape(-1, 8, LANES) for v in values]
    code = scale_of(jnp.concatenate(grouped, axis=0))
    at = 0
    for g in grouped:
        rows = g.shape[0] * 8
        ref[at : at + rows, :] = fixed(g, code).reshape(rows, LANES).astype(I16)
        at += rows
    ref[at : at + 16, :] = jnp.concatenate([code, code], axis=0).astype(I16)


def decode(ref, parts):
    rows = (ref.shape[0] - 16) // parts
    code = ref[parts * rows :, :].astype(I32)[:8]
    step = jnp.exp((code - 15 * PER).astype(F32) * LN)[None]
    out = []
    for p in range(parts):
        q = ref[p * rows : (p + 1) * rows, :].astype(I32).astype(F32)
        out.append((q.reshape(-1, 8, LANES) * step).reshape(rows, LANES))
    return out


def kernel(
    amp_ref, int_ref, rest_ref, occ_ref, virt_ref, sizes_ref, order_ref, out_ref,
    slots, rest_in, rest_slots, a_own, a_oth, v_own, v_oth, part, relay_out, relay_in, main_out, main_in, lad_out, lad_in, upd,
    zs, zr, ys, yr, cs, cr, vs, vr, vl, rl, xs, xr, rs, rr,
):
    rep, tensor = lax.axis_index("rep"), lax.axis_index("tensor")
    x, core = rep // 2, rep % 2
    z, y = tensor // NY, tensor % NY
    width = amp_ref.shape[1]
    rows = amp_ref.shape[0] // NZ
    few = rows // PARTS
    block = few * NZ
    half = block // 2
    piece = width // NY

    def at_x(step):
        return lax.rem(x + step + NX, NX) * 2 + core

    def at_y(step):
        return z * NY + lax.rem(y + step + NY, NY)

    other = x * 2 + 1 - core

    def copy(src, dst, send, recv, to_rep, to_tensor):
        return pltpu.make_async_remote_copy(
            src_ref=src, dst_ref=dst, send_sem=send, recv_sem=recv,
            device_id=(to_rep, to_tensor), device_id_type=MESH,
        )

    barrier = pltpu.get_barrier_semaphore()

    def peer(dz, dy):
        return lax.rem(z + dz, NZ) * NY + lax.rem(y + dy, NY)

    for dz in range(NZ):
        for dy in range(NY):
            if dz or dy:
                pl.semaphore_signal(barrier, inc=1, device_id=(rep, peer(dz, dy)), device_id_type=MESH)
    for to in (at_x(1), at_x(-1), other):
        pl.semaphore_signal(barrier, inc=1, device_id=(to, tensor), device_id_type=MESH)

    v_local = pltpu.make_async_copy(int_ref.at[:, core], v_own, vl)
    v_local.start()
    rest_local = pltpu.make_async_copy(rest_ref, rest_in, rl)
    rest_local.start()

    def pick(b):
        down = lax.broadcasted_iota(I32, (block, 1), 0)
        source = jnp.zeros((block, 1), I32)
        for k in range(NZ):
            source = jnp.where(down // few == k, (down - k * few + b * few) * NZ + order_ref[k], source)
        return jnp.where(lax.broadcasted_iota(I32, (block, rows * NZ), 1) == source, 1.0, 0.0).astype(BF16)

    column = rep * width + lax.broadcasted_iota(I32, (few, width), 1)

    def z_send(b):
        moved = jnp.dot(pick(b), amp_ref[...], preferred_element_type=F32)
        for k in range(NZ):
            kept = jnp.where(column < sizes_ref[order_ref[k]], moved[k * few : (k + 1) * few], 0.0)
            slots[b, k] = kept.astype(BF16)
        if b == 0:
            pl.semaphore_wait(barrier, NZ * NY - 1 + 3)
        here = pl.ds(pl.multiple_of(z * few, few), few)
        for dz in (4, 3, 5, 2, 6, 1, 7):
            to = lax.rem(z + dz, NZ)
            c = copy(slots.at[b, to], a_own.at[0, b, here], zs.at[b, dz], zr.at[b, dz], rep, to * NY + y)
            c.start()
            z_copies[b].append(c)
        a_own[0, b, here, :] = slots[b, z]

    z_copies = [[] for _ in range(PARTS)]
    for b in range(PARTS):
        z_send(b)
    v_copy = copy(int_ref.at[:, 1 - core], v_oth, vs, vr, other, tensor)
    v_copy.start()

    rest_local.wait()
    for b in range(PARTS):
        moved = jnp.dot(pick(b), rest_in[...], preferred_element_type=F32).astype(BF16)
        for k in range(NZ):
            rest_slots[b, k] = moved[k * few : (k + 1) * few]
    eye = lax.broadcasted_iota(I32, (rows, rows), 0) == lax.broadcasted_iota(I32, (rows, rows), 1)
    occ = jnp.sum(jnp.where(eye, occ_ref[...], 0.0), axis=1, keepdims=True)

    upper, lower = pl.ds(0, half), pl.ds(half, half)
    y_copies, c_copies, x_copies, r_copies = {}, {}, {}, {}
    for b in range(PARTS):
        y_copies[b] = [
            copy(a_own.at[0, b], a_own.at[3, b], ys.at[b, 0], yr.at[b, 0], rep, at_y(1)),
            copy(a_own.at[0, b], a_own.at[1, b], ys.at[b, 1], yr.at[b, 1], rep, at_y(-1)),
            copy(a_own.at[3, b, upper], a_own.at[2, b, upper], ys.at[b, 2], yr.at[b, 2], rep, at_y(1)),
            copy(a_own.at[1, b, lower], a_own.at[2, b, lower], ys.at[b, 3], yr.at[b, 3], rep, at_y(-1)),
        ]
        for d in range(NY):
            c_copies[d, b] = copy(a_own.at[d, b], a_oth.at[d, b], cs.at[d, b], cr.at[d, b], other, tensor)
            s, r = xs.at[d, b], xr.at[d, b]
            x_copies[d, b] = [
                copy(relay_out.at[d, b, 0], relay_in.at[d, b, 0], s.at[0], r.at[0], at_x(1), tensor),
                copy(relay_out.at[d, b, 1], relay_in.at[d, b, 1], s.at[1], r.at[1], at_x(-1), tensor),
                copy(main_out.at[d, b, 0], main_in.at[d, b, 0], s.at[2], r.at[2], at_x(1), tensor),
                copy(main_out.at[d, b, 1], main_in.at[d, b, 1], s.at[3], r.at[3], at_x(-1), tensor),
            ]

    left, right = slice(0, LANES), slice(LANES, 2 * LANES)

    def multiply(d, b, s):
        t = lax.rem(x + s, NX)
        part[d, b, s] = dot_t(a_own[d, b], v_own[t]) + dot_t(a_oth[d, b], v_oth[t])

    def stage1(d, b):
        c_copies[d, b].wait_recv()
        multiply(d, b, 2)
        encode(relay_out.at[d, b, 0], [part[d, b, 2, :, left]])
        x_copies[d, b][0].start()
        encode(relay_out.at[d, b, 1], [part[d, b, 2, :, right]])
        x_copies[d, b][1].start()
        for s in (1, 3, 0):
            multiply(d, b, s)

    def stage2(d, b):
        for i, s, into, rest_of in ((0, 1, left, right), (1, 3, right, left)):
            encode(main_out.at[d, b, i, 1 - i], [part[d, b, s, :, rest_of]])
            x_copies[d, b][i].wait_recv()
            [more] = decode(relay_in.at[d, b, i], 1)
            encode(main_out.at[d, b, i, i], [part[d, b, s, :, into] + more])
            x_copies[d, b][2 + i].start()

    def stage3(d, b):
        x_copies[d, b][2].wait_recv()
        x_copies[d, b][3].wait_recv()
        for h, cols in ((0, left), (1, right)):
            [one], [two] = decode(main_in.at[d, b, 0, h], 1), decode(main_in.at[d, b, 1, h], 1)
            part[d, b, 0, :, cols] = part[d, b, 0, :, cols] + one + two
        for dz in range(NZ):
            to = lax.rem(z + dz, NZ)
            here = pl.ds(pl.multiple_of(to * few, few), few)
            whole = part[d, b, 0, here, :]
            encode(lad_out.at[d, b, dz], [whole[:, left], whole[:, right]])
            if dz or d:
                c = copy(
                    lad_out.at[d, b, dz], lad_in.at[b, dz, d], rs.at[b, dz, d], rr.at[b, dz, d], rep, peer(dz, d)
                )
                c.start()
                r_copies[d, b, dz] = c

    def owner(d, b):
        c = lax.rem(y - d + NY, NY)
        cols = pl.ds(pl.multiple_of(c * piece, piece), piece)
        for dz in range(NZ):
            if dz or d:
                r_copies[d, b, dz].wait_recv()
            ladder = jnp.concatenate(decode(lad_in.at[b, dz, d] if dz or d else lad_out.at[d, b, dz], 2), axis=1)
            k = lax.rem(z - dz + NZ, NZ)
            sector = order_ref[k]
            virt = virt_ref[pl.ds(sector, 1), cols]
            new = (ladder + rest_slots[b, k, :, cols].astype(F32)) / (occ[b * few : (b + 1) * few] - virt)
            where = rep * width + c * piece + lax.broadcasted_iota(I32, (few, piece), 1)
            new = jnp.where(where < sizes_ref[sector], new, 0.0)
            upd[pl.ds(pl.multiple_of(b * block + k * few, few), few), cols] = new.astype(BF16)

    def y_send(b):
        for c in z_copies[b]:
            c.wait_recv()
        y_copies[b][0].start()
        y_copies[b][1].start()
        c_copies[0, b].start()

    def y_forward(b):
        y_copies[b][0].wait_recv()
        y_copies[b][2].start()
        c_copies[3, b].start()
        y_copies[b][1].wait_recv()
        y_copies[b][3].start()
        c_copies[1, b].start()

    def y_last(b):
        y_copies[b][2].wait_recv()
        y_copies[b][3].wait_recv()
        c_copies[2, b].start()

    y_send(0)
    v_local.wait()
    v_copy.wait_recv()
    stage1(0, 0)
    stage2(0, 0)
    y_send(1)
    y_forward(0)
    stage3(0, 0)
    stage1(0, 1)
    stage1(3, 0)
    stage2(0, 1)
    stage1(1, 0)
    stage2(3, 0)
    stage3(0, 1)
    stage2(1, 0)
    stage3(3, 0)
    y_forward(1)
    stage3(1, 0)
    stage1(3, 1)
    stage1(1, 1)
    stage2(3, 1)
    y_last(0)
    stage2(1, 1)
    stage1(2, 0)
    stage3(3, 1)
    stage2(2, 0)
    owner(0, 0)
    stage3(1, 1)
    owner(0, 1)
    y_last(1)
    stage1(2, 1)
    stage3(2, 0)
    owner(3, 0)
    stage2(2, 1)
    owner(1, 0)
    owner(3, 1)
    stage3(2, 1)
    owner(1, 1)
    owner(2, 0)
    owner(2, 1)

    wide = lax.broadcasted_iota(I32, (1, rows * NZ), 1)
    lane = jnp.zeros((1, rows * NZ), I32)
    for b in range(PARTS):
        for k in range(NZ):
            first = b * block + k * few
            lane = jnp.where(wide // few == b * NZ + k, (wide - first + b * few) * NZ + order_ref[k], lane)
    back = jnp.where(lax.broadcasted_iota(I32, (rows * NZ, rows * NZ), 0) == lane, 1.0, 0.0).astype(BF16)
    out_ref[...] = jnp.dot(back, upd[...], preferred_element_type=F32).astype(BF16)

    v_copy.wait_send()
    for group in z_copies + list(y_copies.values()) + list(x_copies.values()):
        for c in group:
            c.wait_send()
    for c in list(c_copies.values()) + list(r_copies.values()):
        c.wait_send()


def on_device(amplitudes, integrals, rest, occ_energy, virt_energy, sizes, order):
    rows, groups, width = amplitudes.shape
    piece = width // NY
    few = rows // PARTS
    block = few * groups
    coded = block + 16
    vmem, smem, where_it_is = (pl.BlockSpec(memory_space=m) for m in (pltpu.VMEM, pltpu.SMEM, pl.ANY))
    dma = pltpu.SemaphoreType.DMA
    out = pl.pallas_call(
        kernel,
        out_shape=jax.ShapeDtypeStruct((rows * groups, width), BF16),
        in_specs=[vmem, where_it_is, where_it_is, vmem, vmem, smem, smem],
        out_specs=vmem,
        scratch_shapes=[
            pltpu.VMEM((PARTS, NZ, few, width), BF16),
            pltpu.VMEM((rows * groups, width), BF16),
            pltpu.VMEM((PARTS, NZ, few, width), BF16),
            pltpu.VMEM((NY, PARTS, block, width), BF16),
            pltpu.VMEM((NY, PARTS, block, width), BF16),
            pltpu.VMEM((NX, piece, width), BF16),
            pltpu.VMEM((NX, piece, width), BF16),
            pltpu.VMEM((NY, PARTS, NX, block, piece), F32),
            pltpu.VMEM((NY, PARTS, 2, coded, LANES), I16),
            pltpu.VMEM((NY, PARTS, 2, coded, LANES), I16),
            pltpu.VMEM((NY, PARTS, 2, 2, coded, LANES), I16),
            pltpu.VMEM((NY, PARTS, 2, 2, coded, LANES), I16),
            pltpu.VMEM((NY, PARTS, NZ, 2 * few + 16, LANES), I16),
            pltpu.VMEM((PARTS, NZ, NY, 2 * few + 16, LANES), I16),
            pltpu.VMEM((rows * groups, width), BF16),
            dma((PARTS, NZ)), dma((PARTS, NZ)), dma((PARTS, 4)), dma((PARTS, 4)), dma((NY, PARTS)), dma((NY, PARTS)),
            dma(()), dma(()), dma(()), dma(()),
            dma((NY, PARTS, 4)), dma((NY, PARTS, 4)), dma((PARTS, NZ, NY)), dma((PARTS, NZ, NY)),
        ],
        compiler_params=pltpu.CompilerParams(
            collective_id=0, has_side_effects=True, vmem_limit_bytes=56 * 2**20
        ),
        cost_estimate=pl.CostEstimate(flops=2 * 2048 * 2048 * 1024, bytes_accessed=8 << 20, transcendentals=0),
    )(
        amplitudes.reshape(rows * groups, width),
        integrals.reshape(NX, 2, piece, width),
        rest.reshape(rows * groups, width),
        occ_energy.reshape(1, rows),
        virt_energy,
        sizes,
        order,
    )
    return out.reshape(rows, groups, width)


def solution(mesh):
    placed = (
        P("tensor", None, "rep"),
        P("tensor", None, "rep"),
        P("tensor", None, "rep"),
        P("tensor"),
        P(None, "rep"),
        P(),
        P(),
    )
    return jax.shard_map(
        on_device, mesh=mesh, in_specs=placed, out_specs=P("tensor", None, "rep"), check_vma=False
    )
```

```python
import jax
import jax.numpy as jnp
from jax import lax
from jax.experimental import pallas as pl
from jax.experimental.pallas import tpu as pltpu
from jax.sharding import PartitionSpec as P

MESH = pl.DeviceIdType.MESH
NX, NY, NZ = 4, 4, 8
F32, BF16, I16, I32 = jnp.float32, jnp.bfloat16, jnp.int16, jnp.int32
PARTS = 4
GROUPS = ((0, 1), (2, 3))
ORDER = (0, 3, 1, 2)
CHUNKS = ((0,), (1, 2), (3,))
LANES = 128
PER = 16
LN = 0.6931471805599453 / PER


def dot_t(a, b):
    return lax.dot_general(a, b, (((1,), (1,)), ((), ())), preferred_element_type=F32)


def scale_of(grouped):
    most = jnp.maximum(jnp.max(jnp.abs(grouped), axis=0), 1e-30)
    return (jnp.log(most) * (1 / LN) + (128 * PER + 1.02)).astype(I32) - 128 * PER


def scale_up(code):
    return jnp.exp((15 * PER - code).astype(F32) * LN)


def scale_down(code):
    return jnp.exp((code - 15 * PER).astype(F32) * LN)


def fixed(grouped, code):
    return (grouped * scale_up(code)[None] + 32768.5).astype(I32) - 32768


def encode(ref, values):
    grouped = [v.reshape(-1, 8, LANES) for v in values]
    code = scale_of(jnp.concatenate(grouped, axis=0))
    at = 0
    for g in grouped:
        rows = g.shape[0] * 8
        ref[at : at + rows, :] = fixed(g, code).reshape(rows, LANES).astype(I16)
        at += rows
    ref[at : at + 16, :] = jnp.concatenate([code, code], axis=0).astype(I16)


def decode(ref, parts):
    rows = (ref.shape[0] - 16) // parts
    code = ref[parts * rows :, :].astype(I32)[:8]
    step = scale_down(code)[None]
    out = []
    for p in range(parts):
        q = ref[p * rows : (p + 1) * rows, :].astype(I32).astype(F32)
        out.append((q.reshape(-1, 8, LANES) * step).reshape(rows, LANES))
    return out


def kernel(
    amp_ref, int_ref, rest_ref, occ_ref, virt_ref, sizes_ref, order_ref, out_ref,
    slots, rest_in, rest_slots, a_own, a_oth, v_own, v_oth, part, relay_out, relay_in, main_out, main_in, lad_out, lad_in, upd,
    zs, zr, ys, yr, cs, cr, vs, vr, vl, rl, xs, xr, rs, rr,
):
    rep, tensor = lax.axis_index("rep"), lax.axis_index("tensor")
    x, core = rep // 2, rep % 2
    z, y = tensor // NY, tensor % NY
    width = amp_ref.shape[1]
    rows = amp_ref.shape[0] // NZ
    few = rows // PARTS
    block = few * NZ
    half = block // 2
    piece = width // NY

    def at_x(step):
        return lax.rem(x + step + NX, NX) * 2 + core

    def at_y(step):
        return z * NY + lax.rem(y + step + NY, NY)

    other = x * 2 + 1 - core

    def copy(src, dst, send, recv, to_rep, to_tensor):
        return pltpu.make_async_remote_copy(
            src_ref=src, dst_ref=dst, send_sem=send, recv_sem=recv,
            device_id=(to_rep, to_tensor), device_id_type=MESH,
        )

    barrier = pltpu.get_barrier_semaphore()

    def peer(dz, dy):
        return lax.rem(z + dz, NZ) * NY + lax.rem(y + dy, NY)

    for dz in range(NZ):
        for dy in range(NY):
            if dz or dy:
                pl.semaphore_signal(barrier, inc=1, device_id=(rep, peer(dz, dy)), device_id_type=MESH)
    for to in (at_x(1), at_x(-1), other):
        pl.semaphore_signal(barrier, inc=1, device_id=(to, tensor), device_id_type=MESH)

    v_local = pltpu.make_async_copy(int_ref.at[:, core], v_own, vl)
    v_local.start()
    rest_local = pltpu.make_async_copy(rest_ref, rest_in, rl)
    rest_local.start()

    def pick(b):
        down = lax.broadcasted_iota(I32, (block, 1), 0)
        source = jnp.zeros((block, 1), I32)
        for k in range(NZ):
            source = jnp.where(down // few == k, (down - k * few + b * few) * NZ + order_ref[k], source)
        return jnp.where(lax.broadcasted_iota(I32, (block, rows * NZ), 1) == source, 1.0, 0.0).astype(BF16)

    column = rep * width + lax.broadcasted_iota(I32, (few, width), 1)

    def z_send(b):
        moved = jnp.dot(pick(b), amp_ref[...], preferred_element_type=F32)
        for k in range(NZ):
            kept = jnp.where(column < sizes_ref[order_ref[k]], moved[k * few : (k + 1) * few], 0.0)
            slots[b, k] = kept.astype(BF16)
        if b == 0:
            pl.semaphore_wait(barrier, NZ * NY - 1 + 3)
        here = pl.ds(pl.multiple_of(z * few, few), few)
        for dz in (4, 3, 5, 2, 6, 1, 7):
            to = lax.rem(z + dz, NZ)
            c = copy(slots.at[b, to], a_own.at[b, 0, here], zs.at[b, dz], zr.at[b, dz], rep, to * NY + y)
            c.start()
            z_copies[b].append(c)
        a_own[b, 0, here, :] = slots[b, z]

    z_copies = [[] for _ in range(PARTS)]
    for b in range(PARTS):
        z_send(b)
    v_copy = copy(int_ref.at[:, 1 - core], v_oth, vs, vr, other, tensor)
    v_copy.start()

    rest_local.wait()
    for b in range(PARTS):
        moved = jnp.dot(pick(b), rest_in[...], preferred_element_type=F32).astype(BF16)
        for k in range(NZ):
            rest_slots[b, k] = moved[k * few : (k + 1) * few]
    eye = lax.broadcasted_iota(I32, (rows, rows), 0) == lax.broadcasted_iota(I32, (rows, rows), 1)
    occ = jnp.sum(jnp.where(eye, occ_ref[...], 0.0), axis=1, keepdims=True)

    upper, lower = pl.ds(0, half), pl.ds(half, half)
    y_copies, c_copies, x_copies, r_copies = {}, {}, {}, {}
    for b in range(PARTS):
        own = a_own.at[b]
        y_copies[b] = [
            copy(own.at[0], own.at[1], ys.at[b, 0], yr.at[b, 0], rep, at_y(1)),
            copy(own.at[0], own.at[2], ys.at[b, 1], yr.at[b, 1], rep, at_y(-1)),
            copy(own.at[1, upper], own.at[3, upper], ys.at[b, 2], yr.at[b, 2], rep, at_y(1)),
            copy(own.at[2, lower], own.at[3, lower], ys.at[b, 3], yr.at[b, 3], rep, at_y(-1)),
        ]
        for n in range(NY):
            c_copies[n, b] = copy(own.at[n], a_oth.at[b, n], cs.at[n, b], cr.at[n, b], other, tensor)
        for h in range(len(CHUNKS)):
            s, r, use = xs.at[h, b], xr.at[h, b], pl.ds(0, len(CHUNKS[h]) * block + 16)
            x_copies[h, b] = [
                copy(relay_out.at[h, b, 0, use], relay_in.at[h, b, 0, use], s.at[0], r.at[0], at_x(1), tensor),
                copy(relay_out.at[h, b, 1, use], relay_in.at[h, b, 1, use], s.at[1], r.at[1], at_x(-1), tensor),
                copy(main_out.at[h, b, 0, :, use], main_in.at[h, b, 0, :, use], s.at[2], r.at[2], at_x(1), tensor),
                copy(main_out.at[h, b, 1, :, use], main_in.at[h, b, 1, :, use], s.at[3], r.at[3], at_x(-1), tensor),
            ]

    left, right = slice(0, LANES), slice(LANES, 2 * LANES)

    def span(h):
        first, last = CHUNKS[h][0], CHUNKS[h][-1]
        return slice(first * block, (last + 1) * block)

    def multiply(h, b, s):
        t = lax.rem(x + s, NX)
        here = slice(CHUNKS[h][0], CHUNKS[h][-1] + 1)
        mine = a_own[b, here].reshape(-1, width)
        others = a_oth[b, here].reshape(-1, width)
        part[b, s, span(h)] = dot_t(mine, v_own[t]) + dot_t(others, v_oth[t])

    def stage1(h, b):
        for n in CHUNKS[h]:
            c_copies[n, b].wait_recv()
        multiply(h, b, 2)
        encode(relay_out.at[h, b, 0], [part[b, 2, span(h), left]])
        x_copies[h, b][0].start()
        encode(relay_out.at[h, b, 1], [part[b, 2, span(h), right]])
        x_copies[h, b][1].start()
        for s in (1, 3, 0):
            multiply(h, b, s)

    def stage2(h, b):
        use = pl.ds(0, len(CHUNKS[h]) * block + 16)
        for i, s, into, rest_of in ((0, 1, left, right), (1, 3, right, left)):
            encode(main_out.at[h, b, i, 1 - i], [part[b, s, span(h), rest_of]])
            x_copies[h, b][i].wait_recv()
            [more] = decode(relay_in.at[h, b, i, use], 1)
            encode(main_out.at[h, b, i, i], [part[b, s, span(h), into] + more])
            x_copies[h, b][2 + i].start()

    def stage3(h, b):
        use = pl.ds(0, len(CHUNKS[h]) * block + 16)
        x_copies[h, b][2].wait_recv()
        x_copies[h, b][3].wait_recv()
        for i, cols in ((0, left), (1, right)):
            [one], [two] = decode(main_in.at[h, b, 0, i, use], 1), decode(main_in.at[h, b, 1, i, use], 1)
            part[b, 0, span(h), cols] = part[b, 0, span(h), cols] + one + two

    def give_back(h, g):
        parts = len(GROUPS[g])
        tall = pl.ds(0, 2 * parts * few + 16)
        for n in CHUNKS[h]:
            d = ORDER[n]
            here = slice(n * block, (n + 1) * block)
            values = [
                part[b, 0, here, cols].reshape(NZ, few // 8, 8, LANES) for b in GROUPS[g] for cols in (left, right)
            ]
            code = scale_of(jnp.concatenate([jnp.swapaxes(v, 0, 1) for v in values], axis=0))
            up = scale_up(code)[:, None]
            for i, v in enumerate(values):
                q = ((v * up + 32768.5).astype(I32) - 32768).reshape(NZ, few, LANES)
                lad_out[g, d, :, i * few : (i + 1) * few, :] = q.astype(I16)
            lad_out[g, d, :, 2 * parts * few : 2 * parts * few + 16, :] = jnp.concatenate([code, code], axis=1).astype(I16)
            for dz in range(NZ):
                to = lax.rem(z + dz, NZ)
                if dz or d:
                    c = copy(
                        lad_out.at[g, d, to, tall], lad_in.at[g, d, z, tall],
                        rs.at[g, dz, d], rr.at[g, dz, d], rep, peer(dz, d)
                    )
                    c.start()
                    r_copies[g, dz, d] = c
                else:
                    lad_in[g, d, pl.ds(z, 1)] = lad_out[g, d, pl.ds(z, 1)]

    def owner(h, g):
        parts = len(GROUPS[g])
        for n in CHUNKS[h]:
            d = ORDER[n]
            c = lax.rem(y - d + NY, NY)
            cols = pl.ds(pl.multiple_of(c * piece, piece), piece)
            where = rep * width + c * piece + lax.broadcasted_iota(I32, (few, piece), 1)
            for dz in range(NZ):
                if dz or d:
                    r_copies[g, dz, d].wait_recv()
            code = lad_in[g, d, :, 2 * parts * few : 2 * parts * few + 16, :].astype(I32)[:, :8]
            step = scale_down(code)[:, None]
            for p, b in enumerate(GROUPS[g]):
                ladder = []
                for i in (2 * p, 2 * p + 1):
                    q = lad_in[g, d, :, i * few : (i + 1) * few, :].astype(I32).astype(F32)
                    ladder.append((q.reshape(NZ, few // 8, 8, LANES) * step).reshape(NZ, few, LANES))
                for k in range(NZ):
                    total = jnp.concatenate([ladder[0][k], ladder[1][k]], axis=1) + rest_slots[b, k, :, cols].astype(F32)
                    sector = order_ref[k]
                    virt = virt_ref[pl.ds(sector, 1), cols]
                    new = total / (occ[b * few : (b + 1) * few] - virt)
                    new = jnp.where(where < sizes_ref[sector], new, 0.0)
                    upd[b * block + k * few : b * block + (k + 1) * few, cols] = new.astype(BF16)

    def y_send(b):
        for c in z_copies[b]:
            c.wait_recv()
        y_copies[b][0].start()
        y_copies[b][1].start()
        c_copies[0, b].start()

    def y_forward(b):
        y_copies[b][0].wait_recv()
        y_copies[b][2].start()
        c_copies[1, b].start()
        y_copies[b][1].wait_recv()
        y_copies[b][3].start()
        c_copies[2, b].start()

    def y_last(b):
        y_copies[b][2].wait_recv()
        y_copies[b][3].wait_recv()
        c_copies[3, b].start()

    y_send(0)
    v_local.wait()
    v_copy.wait_recv()
    stage1(0, 0)
    y_send(1)
    y_forward(0)
    stage2(0, 0)
    stage1(0, 1)
    y_send(2)
    stage1(1, 0)
    stage2(0, 1)
    y_forward(1)
    stage1(0, 2)
    stage2(1, 0)
    y_send(3)
    stage1(1, 1)
    y_last(0)
    stage2(0, 2)
    stage1(0, 3)
    y_forward(2)
    stage1(2, 0)
    stage2(1, 1)
    y_last(1)
    stage3(0, 0)
    stage3(0, 1)
    stage2(0, 3)
    stage3(1, 0)
    give_back(0, 0)
    stage1(2, 1)
    stage2(2, 0)
    stage3(1, 1)
    give_back(1, 0)
    y_forward(3)
    stage1(1, 2)
    stage2(2, 1)
    stage1(1, 3)
    stage2(1, 2)
    stage3(2, 0)
    stage3(2, 1)
    y_last(2)
    give_back(2, 0)
    stage3(0, 2)
    stage2(1, 3)
    owner(0, 0)
    stage3(0, 3)
    y_last(3)
    give_back(0, 1)
    stage1(2, 2)
    stage3(1, 2)
    owner(1, 0)
    stage1(2, 3)
    stage3(1, 3)
    give_back(1, 1)
    stage2(2, 2)
    stage2(2, 3)
    owner(2, 0)
    stage3(2, 2)
    stage3(2, 3)
    give_back(2, 1)
    owner(1, 1)
    owner(0, 1)
    owner(2, 1)

    wide = lax.broadcasted_iota(I32, (1, rows * NZ), 1)
    lane = jnp.zeros((1, rows * NZ), I32)
    for b in range(PARTS):
        for k in range(NZ):
            first = b * block + k * few
            lane = jnp.where(wide // few == b * NZ + k, (wide - first + b * few) * NZ + order_ref[k], lane)
    back = jnp.where(lax.broadcasted_iota(I32, (rows * NZ, rows * NZ), 0) == lane, 1.0, 0.0).astype(BF16)
    out_ref[...] = jnp.dot(back, upd[...], preferred_element_type=F32).astype(BF16)

    v_copy.wait_send()
    for group in z_copies + list(y_copies.values()) + list(x_copies.values()):
        for c in group:
            c.wait_send()
    for c in list(c_copies.values()) + list(r_copies.values()):
        c.wait_send()


def on_device(amplitudes, integrals, rest, occ_energy, virt_energy, sizes, order):
    rows, groups, width = amplitudes.shape
    piece = width // NY
    few = rows // PARTS
    block = few * groups
    coded = 2 * block + 16
    back = 2 * few * max(len(g) for g in GROUPS) + 16
    vmem, smem, where_it_is = (pl.BlockSpec(memory_space=m) for m in (pltpu.VMEM, pltpu.SMEM, pl.ANY))
    dma = pltpu.SemaphoreType.DMA
    out = pl.pallas_call(
        kernel,
        out_shape=jax.ShapeDtypeStruct((rows * groups, width), BF16),
        in_specs=[vmem, where_it_is, where_it_is, vmem, vmem, smem, smem],
        out_specs=vmem,
        scratch_shapes=[
            pltpu.VMEM((PARTS, NZ, few, width), BF16),
            pltpu.VMEM((rows * groups, width), BF16),
            pltpu.VMEM((PARTS, NZ, few, width), BF16),
            pltpu.VMEM((PARTS, NY, block, width), BF16),
            pltpu.VMEM((PARTS, NY, block, width), BF16),
            pltpu.VMEM((NX, piece, width), BF16),
            pltpu.VMEM((NX, piece, width), BF16),
            pltpu.VMEM((PARTS, NX, NY * block, piece), F32),
            pltpu.VMEM((len(CHUNKS), PARTS, 2, coded, LANES), I16),
            pltpu.VMEM((len(CHUNKS), PARTS, 2, coded, LANES), I16),
            pltpu.VMEM((len(CHUNKS), PARTS, 2, 2, coded, LANES), I16),
            pltpu.VMEM((len(CHUNKS), PARTS, 2, 2, coded, LANES), I16),
            pltpu.VMEM((len(GROUPS), NY, NZ, back, LANES), I16),
            pltpu.VMEM((len(GROUPS), NY, NZ, back, LANES), I16),
            pltpu.VMEM((rows * groups, width), BF16),
            dma((PARTS, NZ)), dma((PARTS, NZ)), dma((PARTS, 4)), dma((PARTS, 4)), dma((NY, PARTS)), dma((NY, PARTS)),
            dma(()), dma(()), dma(()), dma(()),
            dma((len(CHUNKS), PARTS, 4)), dma((len(CHUNKS), PARTS, 4)), dma((len(GROUPS), NZ, NY)), dma((len(GROUPS), NZ, NY)),
        ],
        compiler_params=pltpu.CompilerParams(
            collective_id=0, has_side_effects=True, vmem_limit_bytes=56 * 2**20
        ),
        cost_estimate=pl.CostEstimate(flops=2 * 2048 * 2048 * 1024, bytes_accessed=8 << 20, transcendentals=0),
    )(
        amplitudes.reshape(rows * groups, width),
        integrals.reshape(NX, 2, piece, width),
        rest.reshape(rows * groups, width),
        occ_energy.reshape(1, rows),
        virt_energy,
        sizes,
        order,
    )
    return out.reshape(rows, groups, width)


def solution(mesh):
    placed = (
        P("tensor", None, "rep"),
        P("tensor", None, "rep"),
        P("tensor", None, "rep"),
        P("tensor"),
        P(None, "rep"),
        P(),
        P(),
    )
    return jax.shard_map(
        on_device, mesh=mesh, in_specs=placed, out_specs=P("tensor", None, "rep"), check_vma=False
    )
```

```python
import jax
import jax.numpy as jnp
from jax import lax
from jax.experimental import pallas as pl
from jax.experimental.pallas import tpu as pltpu
from jax.sharding import PartitionSpec as P

MESH = pl.DeviceIdType.MESH
NX, NY, NZ = 4, 4, 8
F32, BF16, I16, I32 = jnp.float32, jnp.bfloat16, jnp.int16, jnp.int32
PARTS = 4
GROUPS = ((0, 1), (2, 3))
ORDER = (0, 3, 1, 2)
CHUNKS = ((0,), (1, 2), (3,))
LANES = 128
PER = 16
LN = 0.6931471805599453 / PER


def dot_t(a, b):
    return lax.dot_general(a, b, (((1,), (1,)), ((), ())), preferred_element_type=F32)


def scale_of(grouped):
    most = jnp.maximum(jnp.max(jnp.abs(grouped), axis=0), 1e-30)
    return (jnp.log(most) * (1 / LN) + (128 * PER + 1.02)).astype(I32) - 128 * PER


def scale_up(code):
    return jnp.exp((15 * PER - code).astype(F32) * LN)


def scale_down(code):
    return jnp.exp((code - 15 * PER).astype(F32) * LN)


def fixed(grouped, code):
    return (grouped * scale_up(code)[None] + 32768.5).astype(I32) - 32768


def encode(ref, values):
    grouped = [v.reshape(-1, 8, LANES) for v in values]
    code = scale_of(jnp.concatenate(grouped, axis=0))
    at = 0
    for g in grouped:
        rows = g.shape[0] * 8
        ref[at : at + rows, :] = fixed(g, code).reshape(rows, LANES).astype(I16)
        at += rows
    ref[at : at + 16, :] = jnp.concatenate([code, code], axis=0).astype(I16)


def decode(ref, parts):
    rows = (ref.shape[0] - 16) // parts
    code = ref[parts * rows :, :].astype(I32)[:8]
    step = scale_down(code)[None]
    out = []
    for p in range(parts):
        q = ref[p * rows : (p + 1) * rows, :].astype(I32).astype(F32)
        out.append((q.reshape(-1, 8, LANES) * step).reshape(rows, LANES))
    return out


def kernel(
    amp_ref, int_ref, rest_ref, occ_ref, virt_ref, sizes_ref, order_ref, out_ref,
    slots, rest_in, rest_slots, a_own, a_oth, v_own, v_oth, part, relay_out, relay_in, main_out, main_in, lad_out, lad_in, upd,
    zs, zr, ys, yr, cs, cr, vs, vr, vl, rl, xs, xr, rs, rr,
):
    rep, tensor = lax.axis_index("rep"), lax.axis_index("tensor")
    x, core = rep // 2, rep % 2
    z, y = tensor // NY, tensor % NY
    width = amp_ref.shape[1]
    rows = amp_ref.shape[0] // NZ
    few = rows // PARTS
    block = few * NZ
    half = block // 2
    piece = width // NY

    def at_x(step):
        return lax.rem(x + step + NX, NX) * 2 + core

    def at_y(step):
        return z * NY + lax.rem(y + step + NY, NY)

    other = x * 2 + 1 - core

    def copy(src, dst, send, recv, to_rep, to_tensor):
        return pltpu.make_async_remote_copy(
            src_ref=src, dst_ref=dst, send_sem=send, recv_sem=recv,
            device_id=(to_rep, to_tensor), device_id_type=MESH,
        )

    barrier = pltpu.get_barrier_semaphore()

    def peer(dz, dy):
        return lax.rem(z + dz, NZ) * NY + lax.rem(y + dy, NY)

    for dz in range(NZ):
        for dy in range(NY):
            if dz or dy:
                pl.semaphore_signal(barrier, inc=1, device_id=(rep, peer(dz, dy)), device_id_type=MESH)
    for to in (at_x(1), at_x(-1), other):
        pl.semaphore_signal(barrier, inc=1, device_id=(to, tensor), device_id_type=MESH)

    v_local = pltpu.make_async_copy(int_ref.at[:, core], v_own, vl)
    v_local.start()
    rest_local = pltpu.make_async_copy(rest_ref, rest_in, rl)
    rest_local.start()

    def pick(b):
        down = lax.broadcasted_iota(I32, (block, 1), 0)
        source = jnp.zeros((block, 1), I32)
        for k in range(NZ):
            source = jnp.where(down // few == k, (down - k * few + b * few) * NZ + order_ref[k], source)
        return jnp.where(lax.broadcasted_iota(I32, (block, rows * NZ), 1) == source, 1.0, 0.0).astype(BF16)

    column = rep * width + lax.broadcasted_iota(I32, (few, width), 1)

    def z_send(b):
        moved = jnp.dot(pick(b), amp_ref[...], preferred_element_type=F32)
        for k in range(NZ):
            kept = jnp.where(column < sizes_ref[order_ref[k]], moved[k * few : (k + 1) * few], 0.0)
            slots[b, k] = kept.astype(BF16)
        if b == 0:
            pl.semaphore_wait(barrier, NZ * NY - 1 + 3)
        here = pl.ds(pl.multiple_of(z * few, few), few)
        for dz in (4, 3, 5, 2, 6, 1, 7):
            to = lax.rem(z + dz, NZ)
            c = copy(slots.at[b, to], a_own.at[b, 0, here], zs.at[b, dz], zr.at[b, dz], rep, to * NY + y)
            c.start()
            z_copies[b].append(c)
        a_own[b, 0, here, :] = slots[b, z]

    z_copies = [[] for _ in range(PARTS)]
    for b in range(PARTS):
        z_send(b)
    v_copy = copy(int_ref.at[:, 1 - core], v_oth, vs, vr, other, tensor)
    v_copy.start()

    rest_local.wait()
    for b in range(PARTS):
        moved = jnp.dot(pick(b), rest_in[...], preferred_element_type=F32).astype(BF16)
        for k in range(NZ):
            rest_slots[b, k] = moved[k * few : (k + 1) * few]
    eye = lax.broadcasted_iota(I32, (rows, rows), 0) == lax.broadcasted_iota(I32, (rows, rows), 1)
    occ = jnp.sum(jnp.where(eye, occ_ref[...], 0.0), axis=1, keepdims=True)

    upper, lower = pl.ds(0, half), pl.ds(half, half)
    y_copies, c_copies, x_copies, r_copies = {}, {}, {}, {}
    for b in range(PARTS):
        own = a_own.at[b]
        y_copies[b] = [
            copy(own.at[0], own.at[1], ys.at[b, 0], yr.at[b, 0], rep, at_y(1)),
            copy(own.at[0], own.at[2], ys.at[b, 1], yr.at[b, 1], rep, at_y(-1)),
            copy(own.at[1, upper], own.at[3, upper], ys.at[b, 2], yr.at[b, 2], rep, at_y(1)),
            copy(own.at[2, lower], own.at[3, lower], ys.at[b, 3], yr.at[b, 3], rep, at_y(-1)),
        ]
        for n in range(NY):
            c_copies[n, b] = copy(own.at[n], a_oth.at[b, n], cs.at[n, b], cr.at[n, b], other, tensor)
        for h in range(len(CHUNKS)):
            s, r, use = xs.at[h, b], xr.at[h, b], pl.ds(0, len(CHUNKS[h]) * block + 16)
            x_copies[h, b] = [
                copy(relay_out.at[h, b, 0, use], relay_in.at[h, b, 0, use], s.at[0], r.at[0], at_x(1), tensor),
                copy(relay_out.at[h, b, 1, use], relay_in.at[h, b, 1, use], s.at[1], r.at[1], at_x(-1), tensor),
                copy(main_out.at[h, b, 0, :, use], main_in.at[h, b, 0, :, use], s.at[2], r.at[2], at_x(1), tensor),
                copy(main_out.at[h, b, 1, :, use], main_in.at[h, b, 1, :, use], s.at[3], r.at[3], at_x(-1), tensor),
            ]

    left, right = slice(0, LANES), slice(LANES, 2 * LANES)

    def span(h):
        first, last = CHUNKS[h][0], CHUNKS[h][-1]
        return slice(first * block, (last + 1) * block)

    def multiply(h, b, s):
        t = lax.rem(x + s, NX)
        here = slice(CHUNKS[h][0], CHUNKS[h][-1] + 1)
        mine = a_own[b, here].reshape(-1, width)
        others = a_oth[b, here].reshape(-1, width)
        part[b, s, span(h)] = dot_t(mine, v_own[t]) + dot_t(others, v_oth[t])

    def stage1(h, b):
        for n in CHUNKS[h]:
            c_copies[n, b].wait_recv()
        multiply(h, b, 2)
        encode(relay_out.at[h, b, 0], [part[b, 2, span(h), left]])
        x_copies[h, b][0].start()
        encode(relay_out.at[h, b, 1], [part[b, 2, span(h), right]])
        x_copies[h, b][1].start()
        for s in (1, 3, 0):
            multiply(h, b, s)

    def stage2(h, b):
        use = pl.ds(0, len(CHUNKS[h]) * block + 16)
        for i, s, into, rest_of in ((0, 1, left, right), (1, 3, right, left)):
            encode(main_out.at[h, b, i, 1 - i], [part[b, s, span(h), rest_of]])
            x_copies[h, b][i].wait_recv()
            [more] = decode(relay_in.at[h, b, i, use], 1)
            encode(main_out.at[h, b, i, i], [part[b, s, span(h), into] + more])
            x_copies[h, b][2 + i].start()

    def stage3(h, b):
        use = pl.ds(0, len(CHUNKS[h]) * block + 16)
        x_copies[h, b][2].wait_recv()
        x_copies[h, b][3].wait_recv()
        for i, cols in ((0, left), (1, right)):
            [one], [two] = decode(main_in.at[h, b, 0, i, use], 1), decode(main_in.at[h, b, 1, i, use], 1)
            part[b, 0, span(h), cols] = part[b, 0, span(h), cols] + one + two

    def give_back(h, g):
        parts = len(GROUPS[g])
        tall = pl.ds(0, 2 * parts * few + 16)
        for n in CHUNKS[h]:
            d = ORDER[n]
            here = slice(n * block, (n + 1) * block)
            values = [
                part[b, 0, here, cols].reshape(NZ, few // 8, 8, LANES) for b in GROUPS[g] for cols in (left, right)
            ]
            code = scale_of(jnp.concatenate([jnp.swapaxes(v, 0, 1) for v in values], axis=0))
            up = scale_up(code)[:, None]
            for i, v in enumerate(values):
                q = ((v * up + 32768.5).astype(I32) - 32768).reshape(NZ, few, LANES)
                lad_out[g, d, :, i * few : (i + 1) * few, :] = q.astype(I16)
            lad_out[g, d, :, 2 * parts * few : 2 * parts * few + 16, :] = jnp.concatenate([code, code], axis=1).astype(I16)
            for dz in range(NZ):
                to = lax.rem(z + dz, NZ)
                if dz or d:
                    c = copy(
                        lad_out.at[g, d, to, tall], lad_in.at[g, d, z, tall],
                        rs.at[g, dz, d], rr.at[g, dz, d], rep, peer(dz, d)
                    )
                    c.start()
                    r_copies[g, dz, d] = c
                else:
                    lad_in[g, d, pl.ds(z, 1)] = lad_out[g, d, pl.ds(z, 1)]

    def owner(h, g):
        parts = len(GROUPS[g])
        for n in CHUNKS[h]:
            d = ORDER[n]
            c = lax.rem(y - d + NY, NY)
            cols = pl.ds(pl.multiple_of(c * piece, piece), piece)
            where = rep * width + c * piece + lax.broadcasted_iota(I32, (few, piece), 1)
            for dz in range(NZ):
                if dz or d:
                    r_copies[g, dz, d].wait_recv()
            code = lad_in[g, d, :, 2 * parts * few : 2 * parts * few + 16, :].astype(I32)[:, :8]
            step = scale_down(code)[:, None]
            for p, b in enumerate(GROUPS[g]):
                ladder = []
                for i in (2 * p, 2 * p + 1):
                    q = lad_in[g, d, :, i * few : (i + 1) * few, :].astype(I32).astype(F32)
                    ladder.append((q.reshape(NZ, few // 8, 8, LANES) * step).reshape(NZ, few, LANES))
                for k in range(NZ):
                    total = jnp.concatenate([ladder[0][k], ladder[1][k]], axis=1) + rest_slots[b, k, :, cols].astype(F32)
                    sector = order_ref[k]
                    virt = virt_ref[pl.ds(sector, 1), cols]
                    new = total / (occ[b * few : (b + 1) * few] - virt)
                    new = jnp.where(where < sizes_ref[sector], new, 0.0)
                    upd[b * block + k * few : b * block + (k + 1) * few, cols] = new.astype(BF16)

    def y_send(b):
        for c in z_copies[b]:
            c.wait_recv()
        y_copies[b][0].start()
        y_copies[b][1].start()
        c_copies[0, b].start()

    def y_forward(b):
        y_copies[b][0].wait_recv()
        y_copies[b][2].start()
        c_copies[1, b].start()
        y_copies[b][1].wait_recv()
        y_copies[b][3].start()
        c_copies[2, b].start()

    def y_last(b):
        y_copies[b][2].wait_recv()
        y_copies[b][3].wait_recv()
        c_copies[3, b].start()

    y_send(0)
    v_local.wait()
    v_copy.wait_recv()
    stage1(0, 0)
    y_send(1)
    y_forward(0)
    stage2(0, 0)
    stage1(0, 1)
    y_send(2)
    stage1(1, 0)
    stage2(0, 1)
    y_forward(1)
    stage1(0, 2)
    stage2(1, 0)
    y_last(0)
    stage3(0, 0)
    y_send(3)
    stage3(0, 1)
    stage1(1, 1)
    stage1(2, 0)
    stage2(0, 2)
    y_forward(2)
    stage1(0, 3)
    stage2(1, 1)
    stage3(1, 0)
    y_last(1)
    give_back(0, 0)
    stage1(1, 2)
    stage2(0, 3)
    stage1(2, 1)
    stage3(1, 1)
    give_back(1, 0)
    y_forward(3)
    stage2(1, 2)
    owner(0, 0)
    stage3(0, 2)
    stage1(1, 3)
    stage2(2, 1)
    y_last(2)
    stage2(2, 0)
    stage3(0, 3)
    give_back(0, 1)
    stage2(1, 3)
    y_last(3)
    stage1(2, 2)
    stage3(2, 1)
    stage3(2, 0)
    give_back(2, 0)
    stage1(2, 3)
    stage3(1, 2)
    stage3(1, 3)
    give_back(1, 1)
    stage2(2, 3)
    stage2(2, 2)
    stage3(2, 3)
    stage3(2, 2)
    give_back(2, 1)
    owner(1, 0)
    owner(0, 1)
    owner(1, 1)
    owner(2, 0)
    owner(2, 1)

    wide = lax.broadcasted_iota(I32, (1, rows * NZ), 1)
    lane = jnp.zeros((1, rows * NZ), I32)
    for b in range(PARTS):
        for k in range(NZ):
            first = b * block + k * few
            lane = jnp.where(wide // few == b * NZ + k, (wide - first + b * few) * NZ + order_ref[k], lane)
    back = jnp.where(lax.broadcasted_iota(I32, (rows * NZ, rows * NZ), 0) == lane, 1.0, 0.0).astype(BF16)
    out_ref[...] = jnp.dot(back, upd[...], preferred_element_type=F32).astype(BF16)

    v_copy.wait_send()
    for group in z_copies + list(y_copies.values()) + list(x_copies.values()):
        for c in group:
            c.wait_send()
    for c in list(c_copies.values()) + list(r_copies.values()):
        c.wait_send()


def on_device(amplitudes, integrals, rest, occ_energy, virt_energy, sizes, order):
    rows, groups, width = amplitudes.shape
    piece = width // NY
    few = rows // PARTS
    block = few * groups
    coded = 2 * block + 16
    back = 2 * few * max(len(g) for g in GROUPS) + 16
    vmem, smem, where_it_is = (pl.BlockSpec(memory_space=m) for m in (pltpu.VMEM, pltpu.SMEM, pl.ANY))
    dma = pltpu.SemaphoreType.DMA
    out = pl.pallas_call(
        kernel,
        out_shape=jax.ShapeDtypeStruct((rows * groups, width), BF16),
        in_specs=[vmem, where_it_is, where_it_is, vmem, vmem, smem, smem],
        out_specs=vmem,
        scratch_shapes=[
            pltpu.VMEM((PARTS, NZ, few, width), BF16),
            pltpu.VMEM((rows * groups, width), BF16),
            pltpu.VMEM((PARTS, NZ, few, width), BF16),
            pltpu.VMEM((PARTS, NY, block, width), BF16),
            pltpu.VMEM((PARTS, NY, block, width), BF16),
            pltpu.VMEM((NX, piece, width), BF16),
            pltpu.VMEM((NX, piece, width), BF16),
            pltpu.VMEM((PARTS, NX, NY * block, piece), F32),
            pltpu.VMEM((len(CHUNKS), PARTS, 2, coded, LANES), I16),
            pltpu.VMEM((len(CHUNKS), PARTS, 2, coded, LANES), I16),
            pltpu.VMEM((len(CHUNKS), PARTS, 2, 2, coded, LANES), I16),
            pltpu.VMEM((len(CHUNKS), PARTS, 2, 2, coded, LANES), I16),
            pltpu.VMEM((len(GROUPS), NY, NZ, back, LANES), I16),
            pltpu.VMEM((len(GROUPS), NY, NZ, back, LANES), I16),
            pltpu.VMEM((rows * groups, width), BF16),
            dma((PARTS, NZ)), dma((PARTS, NZ)), dma((PARTS, 4)), dma((PARTS, 4)), dma((NY, PARTS)), dma((NY, PARTS)),
            dma(()), dma(()), dma(()), dma(()),
            dma((len(CHUNKS), PARTS, 4)), dma((len(CHUNKS), PARTS, 4)), dma((len(GROUPS), NZ, NY)), dma((len(GROUPS), NZ, NY)),
        ],
        compiler_params=pltpu.CompilerParams(
            collective_id=0, has_side_effects=True, vmem_limit_bytes=56 * 2**20
        ),
        cost_estimate=pl.CostEstimate(flops=2 * 2048 * 2048 * 1024, bytes_accessed=8 << 20, transcendentals=0),
    )(
        amplitudes.reshape(rows * groups, width),
        integrals.reshape(NX, 2, piece, width),
        rest.reshape(rows * groups, width),
        occ_energy.reshape(1, rows),
        virt_energy,
        sizes,
        order,
    )
    return out.reshape(rows, groups, width)


def solution(mesh):
    placed = (
        P("tensor", None, "rep"),
        P("tensor", None, "rep"),
        P("tensor", None, "rep"),
        P("tensor"),
        P(None, "rep"),
        P(),
        P(),
    )
    return jax.shard_map(
        on_device, mesh=mesh, in_specs=placed, out_specs=P("tensor", None, "rep"), check_vma=False
    )
```
